256 devices in a mesh: replica: 16 (over y, z_lo), fsdp: 16 (over x, z_hi, core).
Axes of the slice: x: 4, y: 4, z: 8 (z_hi: 2, z_lo: 4; z = z_hi * 4 + z_lo), core: 2. Of those that a mesh axis runs over, the one named last changes fastest.
Arguments:
- local_weights: float32 [16, 5120, 512], P('replica', 'fsdp')
- outer_base: float32 [5120, 512], P('fsdp')
- outer_momentum: float32 [5120, 512], P(('fsdp', 'replica')), may hold values from -4 to 4
- batch: bfloat16 [16, 2, 6144, 5120], P('replica', None, 'fsdp'), may hold values from -6 to 6
- cotangent: bfloat16 [16, 2, 6144, 512], P('replica', None, 'fsdp'), may hold values from -6 to 6
- step: int32 [1], replicated, may hold values from 0 to 4095
- plan: int32 [8], replicated, may hold values from 0 to 3
Outputs:
- new_weights: float32 [16, 5120, 512], P('replica', 'fsdp')
- new_base: float32 [5120, 512], P('fsdp')
- new_momentum: float32 [5120, 512], P(('fsdp', 'replica'))
The draws below stay inside these ranges and needn't reach their ends.
All inputs are finite; a program needn't handle non-finite values. Where the reference program divides by a largest or mean magnitude, that divisor is 1e-20 or more.
Results may differ from the reference program's by a relative error of at most 0.0055.
Values may be sent and summed in bfloat16 or wider, within the bound.
No kernel may reach another device: no remote copies, remote signals or barrier semaphores. Data moves between devices by JAX's collectives and lax.ppermute only.
A program may use at most 128 MiB of HBM per device.

```python
import jax
import jax.numpy as jnp
from jax import lax

D = 5120
VALUE_WIDTH = 512
HEAD_DIM = 128
FRAGMENTS = 4
SCHED_LEN = 8
INNER = 2
TOK_DEV = 384
TOKENS = 6144
N_REPLICA = 16
N_FSDP = 16


def shared_base(key):
    return jax.random.normal(key, (D, VALUE_WIDTH), jnp.float32)


def draw_outer_base(key, part):
    base_values = shared_base(key)
    return base_values


def draw_local_weights(key, part):
    base_values = shared_base(key)
    key = jax.random.fold_in(key, 12)
    drift = jax.random.normal(key, (N_REPLICA, D, VALUE_WIDTH), jnp.float32)
    return base_values[None] + drift


def with_ends(array, rng, least, high):
    extent = array.shape
    place = [jax.random.randint(jax.random.fold_in(rng, axis), (), 0, extent[axis]) for axis in range(len(extent))]
    array = array.at[tuple(place)].set(least)
    longest = extent.index(max(extent))
    place[longest] = (place[longest] + 1) % extent[longest]
    return array.at[tuple(place)].set(high)


def block_levels(rng, extent, split, low, high):
    def one(dim, shards_of):
        draws = jax.random.uniform(jax.random.fold_in(jax.random.fold_in(rng, 6), dim), (shards_of,), jnp.float32, low / len(split), high / len(split))
        return jnp.repeat(jnp.exp(draws), extent[dim] // shards_of).reshape((-1,) + (1,) * (len(extent) - dim - 1))

    factor_of = one(*split[0])
    for cut in split[1:]:
        factor_of = factor_of * one(*cut)
    return factor_of


def noise(rng, dims, deviation, most, cuts=(), kind=jnp.bfloat16):
    values = deviation * jax.random.normal(rng, dims, jnp.float32)
    if cuts:
        values = values * block_levels(rng, dims, cuts, -0.22, 0.18)
    return jnp.clip(values, -most, most).astype(kind)


def setup_inputs(seed: int = 0) -> dict:
    arg_keys = jax.random.split(jax.random.key(seed), 8)
    return {
        "local_weights": draw_local_weights(jax.random.fold_in(arg_keys[7], 71), 0),
        "outer_base": draw_outer_base(jax.random.fold_in(arg_keys[7], 71), 0),
        "outer_momentum": noise(arg_keys[2], (D, VALUE_WIDTH), 0.3, 4.0, ((0, 256),), jnp.float32),
        "batch": noise(arg_keys[3], (N_REPLICA, INNER, TOKENS, D), 1.0, 6.0, ((0, 16), (2, 16))),
        "cotangent": noise(arg_keys[4], (N_REPLICA, INNER, TOKENS, VALUE_WIDTH), 1.0, 6.0, ((0, 16), (2, 16))),
        "step": jax.random.randint(arg_keys[5], (1,), 0, 4096).astype(jnp.int32),
        "plan": with_ends(jax.random.randint(arg_keys[6], (SCHED_LEN,), 0, FRAGMENTS), jax.random.fold_in(arg_keys[6], 1), 0, FRAGMENTS - 1).astype(jnp.int32),
    }


eps_norm = 1e-06
eps_scale = 1e-06
inner_rate = 0.5
outer_rate = 0.7
outer_decay = 0.9
mix_local = 0.5

def pick_fragment(step, plan):
    position = step[0] % SCHED_LEN
    hits = jnp.arange(SCHED_LEN, dtype=jnp.int32) == position
    return jnp.sum(jnp.where(hits, plan, 0)).astype(jnp.int32)

def rate_of(step):
    return outer_rate * 1024.0 / (1024.0 + step[0].astype(jnp.float32))

def normalize(rows):
    values = rows.astype(jnp.float32)
    mean_square = lax.optimization_barrier(jnp.mean(values * values, axis=-1, keepdims=True))
    return (values * lax.rsqrt(mean_square + eps_norm)).astype(jnp.bfloat16)

def silu_slope(values):
    gate_value = jax.nn.sigmoid(values)
    return gate_value * (1.0 + values * (1.0 - gate_value))

def inner_step(weights, batch_rows, cot_rows):
    inv_width = D ** (-0.5)
    normed = normalize(batch_rows)
    values = jnp.dot(normed, weights.astype(jnp.bfloat16), preferred_element_type=jnp.float32) * inv_width
    slopes = (cot_rows.astype(jnp.float32) * silu_slope(values)).astype(jnp.bfloat16)
    normed_groups = normed.reshape(N_FSDP, TOK_DEV, D)
    slope_groups = slopes.reshape(N_FSDP, TOK_DEV, VALUE_WIDTH)

    def add_group(running, pair):
        product = jnp.dot(pair[0].T, pair[1], preferred_element_type=jnp.float32).astype(jnp.bfloat16)
        product = lax.optimization_barrier(product)
        return (running + product.astype(jnp.float32), None)
    gradient, _ = lax.scan(add_group, jnp.zeros((D, VALUE_WIDTH), jnp.float32), (normed_groups, slope_groups))
    return weights - inner_rate * inv_width * gradient

def reference(local_weights, outer_base, outer_momentum, batch, cotangent, step, plan):
    fragment = pick_fragment(step, plan)
    outer_lr = rate_of(step)
    first_col = (fragment * HEAD_DIM).astype(jnp.int32)
    base_cols = lax.dynamic_slice_in_dim(outer_base, first_col, HEAD_DIM, 1)

    def add_replica(running, weights):
        pseudo_grad = base_cols - lax.dynamic_slice_in_dim(weights, first_col, HEAD_DIM, 1)
        block_scale = (lax.optimization_barrier(jnp.max(jnp.abs(pseudo_grad), axis=1, keepdims=True)) + eps_scale).astype(jnp.bfloat16)
        codes = (pseudo_grad / block_scale.astype(jnp.float32)).astype(jnp.bfloat16)
        return (running + codes.astype(jnp.float32) * block_scale.astype(jnp.float32), None)
    running, _ = lax.scan(add_replica, jnp.zeros((D, HEAD_DIM), jnp.float32), local_weights)
    average = running / N_REPLICA
    moment_cols = lax.dynamic_slice_in_dim(outer_momentum, first_col, HEAD_DIM, 1)
    moment_new = outer_decay * moment_cols + average
    base_frag = base_cols - outer_lr * (outer_decay * moment_new + average)
    new_base = lax.dynamic_update_slice_in_dim(outer_base, base_frag, first_col, 1)
    new_momentum = lax.dynamic_update_slice_in_dim(outer_momentum, moment_new, first_col, 1)

    def train(inputs):
        weights, batch_steps, cot_steps = inputs
        for index in range(INNER):
            weights = inner_step(weights, batch_steps[index], cot_steps[index])
        return weights
    trained = lax.map(train, (local_weights, batch, cotangent))
    trained_cols = lax.dynamic_slice_in_dim(trained, first_col, HEAD_DIM, 2)
    blended = mix_local * trained_cols + (1.0 - mix_local) * base_frag[None]
    new_weights = lax.dynamic_update_slice_in_dim(trained, blended, first_col, 2)
    return (new_weights, new_base, new_momentum)
```

```python
import functools

import jax
import jax.numpy as jnp
from jax import lax
from jax.experimental import pallas as pl
from jax.experimental.pallas import tpu as pltpu
from jax.sharding import PartitionSpec as P

D = 5120
HEAD_DIM = 128
SCHED_LEN = 8
INNER = 2
TOK = 384
HALF = 256
CHUNK = 128
CHAINS = HALF // CHUNK
SLAB = 640

eps_norm = 1e-06
eps_scale = 1e-06
inner_rate = 0.5
outer_rate = 0.7
outer_decay = 0.9
mix_local = 0.5
inv_width = D ** (-0.5)


def place(x, z, c):
    return (x * 2 + z) * 2 + c


PLACES = [(x, z, c) for x in range(4) for z in range(2) for c in range(2)]
X_UP = [(place(x, z, c), place((x + 1) % 4, z, c)) for x, z, c in PLACES]
X_DOWN = [(place(x, z, c), place((x - 1) % 4, z, c)) for x, z, c in PLACES]
X_FAR = [(place(x, z, c), place((x + 2) % 4, z, c)) for x, z, c in PLACES]
Z_SWAP = [(place(x, z, c), place(x, 1 - z, c)) for x, z, c in PLACES]
C_SWAP = [(place(x, z, c), place(x, z, 1 - c)) for x, z, c in PLACES]


def send(value, pairs):
    return lax.ppermute(value, "fsdp", pairs)


def pick_fragment(step, plan):
    position = step[0] % SCHED_LEN
    hits = jnp.arange(SCHED_LEN, dtype=jnp.int32) == position
    return jnp.sum(jnp.where(hits, plan, 0))


def rate_of(step):
    return outer_rate * 1024.0 / (1024.0 + step[0].astype(jnp.float32))


def normalize_kernel(rows_ref, out_ref):
    values = rows_ref[0, 0].astype(jnp.float32)
    mean_square = jnp.mean(values * values, axis=-1, keepdims=True)
    out_ref[...] = (values * lax.rsqrt(mean_square + eps_norm)).astype(jnp.bfloat16)


def normalize(batch, index):
    block = 128
    return pl.pallas_call(
        normalize_kernel,
        grid=(TOK // block,),
        in_specs=[pl.BlockSpec((1, 1, block, D), lambda i: (0, index, i, 0))],
        out_specs=pl.BlockSpec((block, D), lambda i: (i, 0)),
        out_shape=jax.ShapeDtypeStruct((TOK, D), jnp.bfloat16),
        compiler_params=pltpu.CompilerParams(vmem_limit_bytes=48 * 2**20),
        cost_estimate=pl.CostEstimate(flops=4 * TOK * D, bytes_accessed=4 * TOK * D, transcendentals=TOK),
        name="normalize",
    )(batch)


OFFSETS = (0, -1, 1, 2)


def train_kernel(
    index, chain, n_own, n_oth, cot_own, cot_oth, w_own, w_below, w_above, w_far, g_own, g_below, g_above, g_far
):
    me = lax.axis_index("fsdp")
    x, z = me // 4, (me // 2) % 2

    def columns(dx, dz):
        slab = 2 * ((x + dx + 4) % 4) + (z + dz) % 2
        return pl.ds(pl.multiple_of(slab * SLAB, SLAB), SLAB)

    def forward(rows):
        total = jnp.zeros((TOK, CHUNK), jnp.float32)
        for dx, piece in zip(OFFSETS, (w_own, w_below, w_above, w_far)):
            for dz in range(2):
                total = total + lax.dot_general(
                    rows[:, columns(dx, dz)],
                    piece[dz],
                    (((1,), (1,)), ((), ())),
                    preferred_element_type=jnp.float32,
                )
        return total * inv_width

    def slopes(rows, cot_ref):
        values = forward(rows)
        gate = jax.nn.sigmoid(values)
        cot = cot_ref[index, :, chain * CHUNK : (chain + 1) * CHUNK].astype(jnp.float32)
        return (cot * (gate * (1.0 + values * (1.0 - gate)))).T.astype(jnp.bfloat16)

    s_own = slopes(n_own, cot_own)
    s_oth = slopes(n_oth, cot_oth)
    for dx, out in zip((2, 1, -1, 0), (g_far, g_above, g_below, g_own)):
        for dz in range(2):
            cols = columns(dx, dz)
            product = jnp.dot(s_own, n_own[:, cols], preferred_element_type=jnp.float32)
            product = product + jnp.dot(s_oth, n_oth[:, cols], preferred_element_type=jnp.float32)
            out[dz] = product.astype(out.dtype)


def train(n_own, n_oth, cot_own, cot_oth, pieces, index, chain):
    two = (2, CHUNK, SLAB)
    vmem = pl.BlockSpec(memory_space=pltpu.VMEM)
    return pl.pallas_call(
        functools.partial(train_kernel, index, chain),
        in_specs=[vmem] * 8,
        out_specs=[vmem] * 4,
        out_shape=[jax.ShapeDtypeStruct(two, jnp.float32)] + [jax.ShapeDtypeStruct(two, jnp.bfloat16)] * 3,
        compiler_params=pltpu.CompilerParams(vmem_limit_bytes=28 * 2**20),
        cost_estimate=pl.CostEstimate(
            flops=8 * TOK * D * CHUNK, bytes_accessed=4 * TOK * D + 20 * D * CHUNK, transcendentals=2 * TOK * CHUNK
        ),
        name="train",
    )(n_own, n_oth, cot_own, cot_oth, *pieces)


def gather(w_half):
    own = w_half.astype(jnp.bfloat16)
    both = jnp.stack([own, send(own, Z_SWAP)])
    return both, send(both, X_UP), send(both, X_DOWN), send(both, X_FAR)


def reduce(g_own, g_below, g_above, g_far):
    total = g_own
    for part, pairs in ((g_far, X_FAR), (g_above, X_UP), (g_below, X_DOWN)):
        total = total + send(part, pairs).astype(jnp.float32)
    return total[0] + send(total[1].astype(jnp.bfloat16), Z_SWAP).astype(jnp.float32)


def on_device(local_weights, outer_base, outer_momentum, batch, cotangent, step, plan):
    fragment = pick_fragment(step, plan)
    outer_lr = rate_of(step)
    first_col = fragment * HEAD_DIM
    weights = local_weights[0]
    core = lax.axis_index("fsdp") % 2
    my_col, other_col = core * HALF, (1 - core) * HALF

    w_mine = lax.dynamic_slice_in_dim(weights, my_col, HALF, 1).T
    w_sent = lax.dynamic_slice_in_dim(weights, other_col, HALF, 1).T
    w_got = send(w_sent, C_SWAP)
    w_all = jnp.where(
        core == 0, jnp.concatenate([w_mine, w_got], axis=1), jnp.concatenate([w_got, w_mine], axis=1)
    )
    cot_mine = lax.dynamic_slice_in_dim(cotangent[0], my_col, HALF, 2)
    cot_got = send(lax.dynamic_slice_in_dim(cotangent[0], other_col, HALF, 2), C_SWAP)
    batch, w_all = lax.optimization_barrier((batch, w_all))
    normed = [normalize(batch, index) for index in range(INNER)]
    normed_got = [send(rows, C_SWAP) for rows in normed]

    base_cols = lax.dynamic_slice_in_dim(outer_base, first_col, HEAD_DIM, 1)
    pseudo_grad = base_cols - lax.dynamic_slice_in_dim(weights, first_col, HEAD_DIM, 1)
    block_scale = (jnp.max(jnp.abs(pseudo_grad), axis=1, keepdims=True) + eps_scale).astype(jnp.bfloat16)
    block_scale = block_scale.astype(jnp.float32)
    codes = (pseudo_grad / block_scale).astype(jnp.bfloat16)
    replicas = lax.axis_size("replica")
    products = (codes.astype(jnp.float32) * block_scale).reshape(replicas, -1, HEAD_DIM)
    average = jnp.sum(lax.all_to_all(products, "replica", 0, 0, tiled=True), axis=0) / replicas
    moment_cols = lax.dynamic_slice_in_dim(outer_momentum, first_col, HEAD_DIM, 1)
    share_rows = moment_cols.shape[0]
    share_first = lax.axis_index("replica") * share_rows
    moment_new = outer_decay * moment_cols + average
    base_share = lax.dynamic_slice_in_dim(base_cols, share_first, share_rows, 0)
    base_share = base_share - outer_lr * (outer_decay * moment_new + average)
    base_frag = lax.all_to_all(
        jnp.broadcast_to(base_share, (replicas, share_rows, HEAD_DIM)), "replica", 0, 0, tiled=True
    ).reshape(-1, HEAD_DIM)
    new_base = lax.dynamic_update_slice_in_dim(outer_base, base_frag, first_col, 1)
    new_momentum = lax.dynamic_update_slice_in_dim(outer_momentum, moment_new, first_col, 1)

    chains = [w_all[k * CHUNK : (k + 1) * CHUNK] for k in range(CHAINS)]
    for index in range(INNER):
        for k in range(CHAINS):
            pieces = gather(chains[k])
            grads = train(normed[index], normed_got[index], cot_mine, cot_got, pieces, index, k)
            chains[k] = chains[k] - inner_rate * inv_width * reduce(*grads)

    rows_of = weights.shape[0]
    mine_cols, other_cols = [], []
    for chain in chains:
        kept = lax.dynamic_slice_in_dim(chain, core * rows_of, rows_of, 1)
        sent = lax.dynamic_slice_in_dim(chain, (1 - core) * rows_of, rows_of, 1)
        mine_cols.append(kept.T)
        other_cols.append(send(sent, C_SWAP).T)
    trained = jnp.where(
        core == 0,
        jnp.concatenate(mine_cols + other_cols, axis=1),
        jnp.concatenate(other_cols + mine_cols, axis=1),
    )
    in_fragment = jnp.arange(trained.shape[1]) // HEAD_DIM == fragment
    base_wide = jnp.tile(base_frag, (1, trained.shape[1] // HEAD_DIM))
    new_weights = jnp.where(in_fragment[None, :], mix_local * trained + (1.0 - mix_local) * base_wide, trained)
    return (new_weights[None], new_base, new_momentum)


def solution(mesh):
    placed = (
        P("replica", "fsdp", None),
        P("fsdp", None),
        P(("fsdp", "replica"), None),
        P("replica", None, "fsdp", None),
        P("replica", None, "fsdp", None),
        P(),
        P(),
    )
    return jax.shard_map(
        on_device,
        mesh=mesh,
        in_specs=placed,
        out_specs=(P("replica", "fsdp", None), P("fsdp", None), P(("fsdp", "replica"), None)),
        check_vma=False,
    )
```

```python
import jax
import jax.numpy as jnp
from jax import lax
from jax.experimental import pallas as pl
from jax.experimental.pallas import tpu as pltpu
from jax.sharding import PartitionSpec as P

D = 5120
HEAD_DIM = 128
SCHED_LEN = 8
INNER = 2
TOK = 384
HALF = 256
SLAB = 640

eps_norm = 1e-06
eps_scale = 1e-06
inner_rate = 0.5
outer_rate = 0.7
outer_decay = 0.9
mix_local = 0.5
inv_width = D ** (-0.5)


def place(x, z, c):
    return (x * 2 + z) * 2 + c


PLACES = [(x, z, c) for x in range(4) for z in range(2) for c in range(2)]
X_UP = [(place(x, z, c), place((x + 1) % 4, z, c)) for x, z, c in PLACES]
X_DOWN = [(place(x, z, c), place((x - 1) % 4, z, c)) for x, z, c in PLACES]
X_FAR = [(place(x, z, c), place((x + 2) % 4, z, c)) for x, z, c in PLACES]
Z_SWAP = [(place(x, z, c), place(x, 1 - z, c)) for x, z, c in PLACES]
C_SWAP = [(place(x, z, c), place(x, z, 1 - c)) for x, z, c in PLACES]


REPLICA_STEPS = [[(r, r ^ bit) for r in range(16)] for bit in (4, 8, 1, 2)]


def send(value, pairs):
    return lax.ppermute(value, "fsdp", pairs)


def in_hbm(value):
    return pltpu.with_memory_space_constraint(value, pltpu.HBM)


def normalize_kernel(rows_ref, out_ref):
    values = rows_ref[0, 0].astype(jnp.float32)
    mean_square = jnp.mean(values * values, axis=-1, keepdims=True)
    out_ref[...] = (values * lax.rsqrt(mean_square + eps_norm)).astype(jnp.bfloat16)


def normalize(batch, index):
    block = 96
    return pl.pallas_call(
        normalize_kernel,
        grid=(TOK // block,),
        in_specs=[pl.BlockSpec((1, 1, block, D), lambda i: (0, index, i, 0))],
        out_specs=pl.BlockSpec((block, D), lambda i: (i, 0)),
        out_shape=jax.ShapeDtypeStruct((TOK, D), jnp.bfloat16),
        compiler_params=pltpu.CompilerParams(vmem_limit_bytes=16 * 2**20),
        cost_estimate=pl.CostEstimate(flops=4 * TOK * D, bytes_accessed=4 * TOK * D, transcendentals=TOK),
        name="normalize",
    )(batch)


def small_call(kernel, n_smem, n_vmem, out_shape, name):
    vmem = pl.BlockSpec(memory_space=pltpu.VMEM)
    return pl.pallas_call(
        kernel,
        in_specs=[pl.BlockSpec(memory_space=pltpu.SMEM)] * n_smem + [vmem] * n_vmem,
        out_specs=[vmem] * len(out_shape),
        out_shape=out_shape,
        compiler_params=pltpu.CompilerParams(vmem_limit_bytes=8 * 2**20),
        name=name,
    )


def f32_shape(*dims):
    return jax.ShapeDtypeStruct(dims, jnp.float32)


def bf16_shape(*dims):
    return jax.ShapeDtypeStruct(dims, jnp.bfloat16)


def my_core():
    return lax.axis_index("fsdp") % 2


def half_columns(core):
    return pl.ds(pl.multiple_of(core * HALF, HALF), HALF)


def fragment_columns(step_ref, plan_ref):
    fragment = plan_ref[lax.rem(step_ref[0], SCHED_LEN)]
    return pl.ds(pl.multiple_of(fragment * HEAD_DIM, HEAD_DIM), HEAD_DIM)


def split_weights_kernel(weights_ref, w_mine, w_sent):
    core = my_core()
    for out, half in ((w_sent, 1 - core), (w_mine, core)):
        out[...] = weights_ref[0, :, half_columns(half)].T


def merge_kernel(w_mine, w_got, whole_ref, rounded_ref):
    for core in range(2):
        low, high = (w_mine, w_got) if core == 0 else (w_got, w_mine)

        @pl.when(my_core() == core)
        def _():
            whole = jnp.concatenate([low[...], high[...]], axis=1)
            whole_ref[...] = whole
            rounded_ref[...] = whole.astype(jnp.bfloat16)


def finish_kernel(w_ref, mine_ref, got_ref, kept_ref, sent_ref):
    gradient = mine_ref[...] + got_ref[...].astype(jnp.float32)
    trained = w_ref[...] - inner_rate * inv_width * gradient
    rows = kept_ref.shape[1]
    for core in range(2):
        low, high = (kept_ref, sent_ref) if core == 0 else (sent_ref, kept_ref)

        @pl.when(my_core() == core)
        def _():
            low[...] = trained[:, :rows]
            high[...] = trained[:, rows:]


def outer_in_kernel(
    step_ref, plan_ref, base_hbm, weights_hbm, momentum_hbm, out_ref, base_ref, weights_ref, momentum_ref, sems
):
    cols = fragment_columns(step_ref, plan_ref)
    copies = [
        pltpu.make_async_copy(base_hbm.at[:, cols], base_ref, sems.at[0]),
        pltpu.make_async_copy(weights_hbm.at[0, :, cols], weights_ref, sems.at[1]),
        pltpu.make_async_copy(momentum_hbm.at[:, cols], momentum_ref, sems.at[2]),
    ]
    for copy in copies:
        copy.start()
    for copy in copies:
        copy.wait()
    replicas = lax.axis_size("replica")
    pseudo_grad = base_ref[...] - weights_ref[...]
    block_scale = (jnp.max(jnp.abs(pseudo_grad), axis=1, keepdims=True) + eps_scale).astype(jnp.bfloat16)
    block_scale = block_scale.astype(jnp.float32)
    codes = (pseudo_grad / block_scale).astype(jnp.bfloat16).astype(jnp.float32)
    products = codes * block_scale * ((1.0 + outer_decay) / replicas)
    moment = outer_decay**2 * momentum_ref[...]
    share = momentum_ref.shape[0]
    mine = lax.axis_index("replica")
    for k in range(replicas):
        rows = slice(k * share, (k + 1) * share)
        out_ref[rows] = products[rows] + jnp.where(mine == k, moment, 0.0)


def outer_in(step, plan, base, weights, momentum):
    rows, share = base.shape[0], momentum.shape[0]
    smem, hbm = pl.BlockSpec(memory_space=pltpu.SMEM), pl.BlockSpec(memory_space=pl.ANY)
    return pl.pallas_call(
        outer_in_kernel,
        in_specs=[smem] * 2 + [hbm] * 3,
        out_specs=pl.BlockSpec(memory_space=pltpu.VMEM),
        out_shape=f32_shape(rows, HEAD_DIM),
        scratch_shapes=[pltpu.VMEM((size, HEAD_DIM), jnp.float32) for size in (rows, rows, share)]
        + [pltpu.SemaphoreType.DMA((3,))],
        compiler_params=pltpu.CompilerParams(vmem_limit_bytes=8 * 2**20),
        name="outer_in",
    )(step, plan, in_hbm(base), in_hbm(weights), in_hbm(momentum))


def outer_out_kernel(step_ref, plan_ref, total_ref, base_ref, momentum_ref, new_base_ref, new_momentum_ref):
    cols = fragment_columns(step_ref, plan_ref)
    rate = outer_rate * 1024.0 / (1024.0 + jnp.full((1, HEAD_DIM), step_ref[0], jnp.int32).astype(jnp.float32))
    new_base_ref[...] = base_ref[...]
    new_base_ref[:, cols] = base_ref[:, cols] - rate * total_ref[...]
    share = momentum_ref.shape[0]
    mine = lax.axis_index("replica")
    total = jnp.zeros((share, HEAD_DIM), jnp.float32)
    for k in range(lax.axis_size("replica")):
        total = jnp.where(mine == k, total_ref[k * share : (k + 1) * share], total)
    moment = momentum_ref[:, cols]
    average = (total - outer_decay**2 * moment) * (1.0 / (1.0 + outer_decay))
    new_momentum_ref[...] = momentum_ref[...]
    new_momentum_ref[:, cols] = outer_decay * moment + average


def join_kernel(step_ref, plan_ref, base_ref, mine_ref, other_ref, out_ref):
    core = my_core()
    out_ref[0, :, half_columns(core)] = mine_ref[...].T
    out_ref[0, :, half_columns(1 - core)] = other_ref[...].T
    cols = fragment_columns(step_ref, plan_ref)
    out_ref[0, :, cols] = mix_local * out_ref[0, :, cols] + (1.0 - mix_local) * base_ref[:, cols]


OFFSETS = (0, -1, 1, 2)


def slab_columns(dx, dz):
    me = lax.axis_index("fsdp")
    slab = 2 * ((me // 4 + dx + 4) % 4) + ((me // 2) % 2 + dz) % 2
    return pl.ds(pl.multiple_of(slab * SLAB, SLAB), SLAB)


def values_of(rows, pieces, dz):
    total = jnp.zeros((TOK, HALF), jnp.float32)
    for dx, piece in zip(OFFSETS, pieces):
        total = total + lax.dot_general(
            rows[:, slab_columns(dx, dz)],
            piece[...],
            (((1,), (1,)), ((), ())),
            preferred_element_type=jnp.float32,
        )
    return total


def gradients(n_own, n_oth, s_own, s_oth, outs, dz):
    for dx, out in reversed(list(zip(OFFSETS, outs))):
        cols = slab_columns(dx, dz)
        product = jnp.dot(s_own, n_own[:, cols], preferred_element_type=jnp.float32)
        product = product + jnp.dot(s_oth, n_oth[:, cols], preferred_element_type=jnp.float32)
        out[...] = product.astype(out.dtype)


def forward_kernel(n_own, n_oth, p0, p1, p2, p3, out_ref):
    out_ref[0] = values_of(n_own, (p0, p1, p2, p3), 0)
    out_ref[1] = values_of(n_oth, (p0, p1, p2, p3), 0)


def turn_kernel(index, n_own, n_oth, cot_own, cot_oth, part_ref, p0, p1, p2, p3, s_own, s_oth, *outs):
    for half, (rows, cot_ref, s_ref) in enumerate(((n_own, cot_own, s_own), (n_oth, cot_oth, s_oth))):
        values = (part_ref[half] + values_of(rows, (p0, p1, p2, p3), 1)) * inv_width
        gate = jax.nn.sigmoid(values)
        cot = cot_ref[0, index, :, half_columns(my_core())].astype(jnp.float32)
        s_ref[...] = (cot * (gate * (1.0 + values * (1.0 - gate)))).T.astype(jnp.bfloat16)
    gradients(n_own, n_oth, s_own[...], s_oth[...], outs, 1)


def backward_kernel(n_own, n_oth, s_own, s_oth, *outs):
    gradients(n_own, n_oth, s_own[...], s_oth[...], outs, 0)


def big_call(kernel, n_vmem, out_shape, name, flops):
    vmem = pl.BlockSpec(memory_space=pltpu.VMEM)
    return pl.pallas_call(
        kernel,
        in_specs=[vmem] * n_vmem,
        out_specs=[vmem] * len(out_shape),
        out_shape=out_shape,
        compiler_params=pltpu.CompilerParams(vmem_limit_bytes=20 * 2**20),
        cost_estimate=pl.CostEstimate(flops=flops, bytes_accessed=2**20, transcendentals=0),
        name=name,
    )


def after(value, *others):
    return lax.optimization_barrier((value, *others))[0]


def spread(piece):
    return piece, send(piece, X_UP), send(piece, X_DOWN), send(piece, X_FAR)


def on_device(local_weights, outer_base, outer_momentum, batch, cotangent, step, plan):
    rows_of, width = outer_base.shape
    rate = inner_rate * inv_width
    slab, slab_bf16, slopes = f32_shape(HALF, SLAB), bf16_shape(HALF, SLAB), bf16_shape(HALF, TOK)

    half_w = f32_shape(HALF, rows_of)
    w_mine, w_sent = small_call(split_weights_kernel, 0, 1, [half_w] * 2, "split_weights")(local_weights)
    w_got = send(w_sent, C_SWAP)
    weights, own = small_call(merge_kernel, 0, 2, [slab, slab_bf16], "merge")(w_mine, w_got)
    batches = (in_hbm(batch), send(after(batch, w_got), C_SWAP))

    def sum_step(total, k):
        return total + lax.ppermute(total, "replica", REPLICA_STEPS[k])

    total = outer_in(step, plan, outer_base, local_weights, outer_momentum)
    for index in range(INNER):
        other = send(own, Z_SWAP)
        pieces = spread(own)
        other = after(other, *pieces[1:])
        if index == 0:
            other = after(other, total, batches[1])
            cots = (cotangent, send(after(cotangent, other), C_SWAP))
        pieces_other = spread(other)
        normed = [normalize(rows, index) for rows in batches]
        part = big_call(forward_kernel, 6, [f32_shape(2, TOK, HALF)], "forward", 8 * TOK * SLAB * HALF)(
            *normed, *pieces
        )[0]
        total = sum_step(after(total, other), 2 * index)
        part = after(part, total)
        s_own, s_oth, *grads_other = big_call(
            lambda *refs, index=index: turn_kernel(index, *refs),
            9,
            [slopes] * 2 + [slab] + [slab_bf16] * 3,
            "turn",
            16 * TOK * SLAB * HALF,
        )(*normed, *cots, part, *pieces_other)
        own_grad, *sent_grads = grads_other
        arrived = [send(grad, pairs) for grad, pairs in zip(sent_grads, (X_DOWN, X_UP, X_FAR))]
        sum_other = sum((piece.astype(jnp.float32) for piece in arrived), own_grad)
        grads = big_call(backward_kernel, 4, [slab] + [slab_bf16] * 3, "backward", 8 * TOK * SLAB * HALF)(
            *normed, s_own, s_oth
        )
        total = sum_step(after(total, s_own), 2 * index + 1)
        sum_other = after(sum_other, total)
        got = send(sum_other.astype(jnp.bfloat16), Z_SWAP)
        below = send(grads[1], X_DOWN)
        above = send(grads[2], X_UP)
        far = send(grads[3], X_FAR)
        mine = sum((piece.astype(jnp.float32) for piece in (below, above, far)), grads[0])
        if index == 0:
            weights = weights - rate * (mine + got.astype(jnp.float32))
            own = weights.astype(jnp.bfloat16)

    new_base, new_momentum = small_call(
        outer_out_kernel, 2, 3, [f32_shape(rows_of, width), f32_shape(*outer_momentum.shape)], "outer_out"
    )(step, plan, total, outer_base, outer_momentum)

    kept, sent = small_call(finish_kernel, 0, 3, [half_w] * 2, "finish")(weights, after(mine, new_base), got)
    new_weights = small_call(join_kernel, 2, 3, [f32_shape(1, rows_of, width)], "join")(
        step, plan, new_base, kept, send(sent, C_SWAP)
    )[0]
    return (new_weights, new_base, new_momentum)


def solution(mesh):
    placed = (
        P("replica", "fsdp", None),
        P("fsdp", None),
        P(("fsdp", "replica"), None),
        P("replica", None, "fsdp", None),
        P("replica", None, "fsdp", None),
        P(),
        P(),
    )
    return jax.shard_map(
        on_device,
        mesh=mesh,
        in_specs=placed,
        out_specs=(P("replica", "fsdp", None), P("fsdp", None), P(("fsdp", "replica"), None)),
        check_vma=False,
    )
```

```python
import jax
import jax.numpy as jnp
from jax import lax
from jax.experimental import pallas as pl
from jax.experimental.pallas import tpu as pltpu
from jax.sharding import PartitionSpec as P

D = 5120
HEAD_DIM = 128
SCHED_LEN = 8
INNER = 2
TOK = 384
HALF = 256
SLAB = 640

eps_norm = 1e-06
eps_scale = 1e-06
inner_rate = 0.5
outer_rate = 0.7
outer_decay = 0.9
mix_local = 0.5
inv_width = D ** (-0.5)


def place(x, z, c):
    return (x * 2 + z) * 2 + c


PLACES = [(x, z, c) for x in range(4) for z in range(2) for c in range(2)]
X_UP = [(place(x, z, c), place((x + 1) % 4, z, c)) for x, z, c in PLACES]
X_DOWN = [(place(x, z, c), place((x - 1) % 4, z, c)) for x, z, c in PLACES]
X_FAR = [(place(x, z, c), place((x + 2) % 4, z, c)) for x, z, c in PLACES]
Z_SWAP = [(place(x, z, c), place(x, 1 - z, c)) for x, z, c in PLACES]
C_SWAP = [(place(x, z, c), place(x, z, 1 - c)) for x, z, c in PLACES]


REPLICA_STEPS = [[(r, r ^ bit) for r in range(16)] for bit in (4, 8, 1, 2)]


def send(value, pairs):
    return lax.ppermute(value, "fsdp", pairs)


def in_hbm(value):
    return pltpu.with_memory_space_constraint(value, pltpu.HBM)


def normalize_kernel(rows_ref, out_ref):
    values = rows_ref[0, 0].astype(jnp.float32)
    mean_square = jnp.mean(values * values, axis=-1, keepdims=True)
    out_ref[...] = (values * lax.rsqrt(mean_square + eps_norm)).astype(jnp.bfloat16)


def normalize(batch, index):
    block = 96
    return pl.pallas_call(
        normalize_kernel,
        grid=(TOK // block,),
        in_specs=[pl.BlockSpec((1, 1, block, D), lambda i: (0, index, i, 0))],
        out_specs=pl.BlockSpec((block, D), lambda i: (i, 0)),
        out_shape=jax.ShapeDtypeStruct((TOK, D), jnp.bfloat16),
        compiler_params=pltpu.CompilerParams(vmem_limit_bytes=16 * 2**20),
        cost_estimate=pl.CostEstimate(flops=4 * TOK * D, bytes_accessed=4 * TOK * D, transcendentals=TOK),
        name="normalize",
    )(batch)


def small_call(kernel, n_smem, n_vmem, out_shape, name):
    vmem = pl.BlockSpec(memory_space=pltpu.VMEM)
    return pl.pallas_call(
        kernel,
        in_specs=[pl.BlockSpec(memory_space=pltpu.SMEM)] * n_smem + [vmem] * n_vmem,
        out_specs=[vmem] * len(out_shape),
        out_shape=out_shape,
        compiler_params=pltpu.CompilerParams(vmem_limit_bytes=8 * 2**20),
        name=name,
    )


def f32_shape(*dims):
    return jax.ShapeDtypeStruct(dims, jnp.float32)


def bf16_shape(*dims):
    return jax.ShapeDtypeStruct(dims, jnp.bfloat16)


def my_core():
    return lax.axis_index("fsdp") % 2


def half_columns(core):
    return pl.ds(pl.multiple_of(core * HALF, HALF), HALF)


def fragment_columns(step_ref, plan_ref):
    fragment = plan_ref[lax.rem(step_ref[0], SCHED_LEN)]
    return pl.ds(pl.multiple_of(fragment * HEAD_DIM, HEAD_DIM), HEAD_DIM)


def split_weights_kernel(weights_ref, w_mine, w_sent):
    core = my_core()
    for out, half in ((w_sent, 1 - core), (w_mine, core)):
        out[...] = weights_ref[0, :, half_columns(half)].T


def merge_kernel(w_mine, w_got, whole_ref, rounded_ref):
    for core in range(2):
        low, high = (w_mine, w_got) if core == 0 else (w_got, w_mine)

        @pl.when(my_core() == core)
        def _():
            whole = jnp.concatenate([low[...], high[...]], axis=1)
            whole_ref[...] = whole
            rounded_ref[...] = whole.astype(jnp.bfloat16)


def finish_kernel(w_ref, mine_ref, got_ref, kept_ref, sent_ref):
    gradient = mine_ref[...] + got_ref[...].astype(jnp.float32)
    trained = w_ref[...] - inner_rate * inv_width * gradient
    rows = kept_ref.shape[1]
    for core in range(2):
        low, high = (kept_ref, sent_ref) if core == 0 else (sent_ref, kept_ref)

        @pl.when(my_core() == core)
        def _():
            low[...] = trained[:, :rows]
            high[...] = trained[:, rows:]


def outer_in_kernel(
    step_ref, plan_ref, base_hbm, weights_hbm, momentum_hbm, out_ref, base_ref, weights_ref, momentum_ref, sems
):
    cols = fragment_columns(step_ref, plan_ref)
    copies = [
        pltpu.make_async_copy(base_hbm.at[:, cols], base_ref, sems.at[0]),
        pltpu.make_async_copy(weights_hbm.at[0, :, cols], weights_ref, sems.at[1]),
        pltpu.make_async_copy(momentum_hbm.at[:, cols], momentum_ref, sems.at[2]),
    ]
    for copy in copies:
        copy.start()
    for copy in copies:
        copy.wait()
    replicas = lax.axis_size("replica")
    pseudo_grad = base_ref[...] - weights_ref[...]
    block_scale = (jnp.max(jnp.abs(pseudo_grad), axis=1, keepdims=True) + eps_scale).astype(jnp.bfloat16)
    block_scale = block_scale.astype(jnp.float32)
    codes = (pseudo_grad / block_scale).astype(jnp.bfloat16).astype(jnp.float32)
    products = codes * block_scale * ((1.0 + outer_decay) / replicas)
    moment = outer_decay**2 * momentum_ref[...]
    share = momentum_ref.shape[0]
    mine = lax.axis_index("replica")
    for k in range(replicas):
        rows = slice(k * share, (k + 1) * share)
        out_ref[rows] = products[rows] + jnp.where(mine == k, moment, 0.0)


def outer_in(step, plan, base, weights, momentum):
    rows, share = base.shape[0], momentum.shape[0]
    smem, hbm = pl.BlockSpec(memory_space=pltpu.SMEM), pl.BlockSpec(memory_space=pl.ANY)
    return pl.pallas_call(
        outer_in_kernel,
        in_specs=[smem] * 2 + [hbm] * 3,
        out_specs=pl.BlockSpec(memory_space=pltpu.VMEM),
        out_shape=f32_shape(rows, HEAD_DIM),
        scratch_shapes=[pltpu.VMEM((size, HEAD_DIM), jnp.float32) for size in (rows, rows, share)]
        + [pltpu.SemaphoreType.DMA((3,))],
        compiler_params=pltpu.CompilerParams(vmem_limit_bytes=8 * 2**20),
        name="outer_in",
    )(step, plan, in_hbm(base), in_hbm(weights), in_hbm(momentum))


def outer_out_kernel(step_ref, plan_ref, total_ref, base_ref, momentum_ref, new_base_ref, new_momentum_ref):
    cols = fragment_columns(step_ref, plan_ref)
    rate = outer_rate * 1024.0 / (1024.0 + jnp.full((1, HEAD_DIM), step_ref[0], jnp.int32).astype(jnp.float32))
    new_base_ref[...] = base_ref[...]
    new_base_ref[:, cols] = base_ref[:, cols] - rate * total_ref[...]
    share = momentum_ref.shape[0]
    mine = lax.axis_index("replica")
    total = jnp.zeros((share, HEAD_DIM), jnp.float32)
    for k in range(lax.axis_size("replica")):
        total = jnp.where(mine == k, total_ref[k * share : (k + 1) * share], total)
    moment = momentum_ref[:, cols]
    average = (total - outer_decay**2 * moment) * (1.0 / (1.0 + outer_decay))
    new_momentum_ref[...] = momentum_ref[...]
    new_momentum_ref[:, cols] = outer_decay * moment + average


def join_kernel(step_ref, plan_ref, base_ref, mine_ref, other_ref, out_ref):
    core = my_core()
    out_ref[0, :, half_columns(core)] = mine_ref[...].T
    out_ref[0, :, half_columns(1 - core)] = other_ref[...].T
    cols = fragment_columns(step_ref, plan_ref)
    out_ref[0, :, cols] = mix_local * out_ref[0, :, cols] + (1.0 - mix_local) * base_ref[:, cols]


OFFSETS = (0, -1, 1, 2)


def slab_columns(dx, dz):
    me = lax.axis_index("fsdp")
    slab = 2 * ((me // 4 + dx + 4) % 4) + ((me // 2) % 2 + dz) % 2
    return pl.ds(pl.multiple_of(slab * SLAB, SLAB), SLAB)


def values_of(rows, pieces, dz):
    total = jnp.zeros((TOK, HALF), jnp.float32)
    for dx, piece in zip(OFFSETS, pieces):
        total = total + lax.dot_general(
            rows[:, slab_columns(dx, dz)],
            piece,
            (((1,), (1,)), ((), ())),
            preferred_element_type=jnp.float32,
        )
    return total


def gradients(n_own, n_oth, s_own, s_oth, outs, dz):
    for dx, out in reversed(list(zip(OFFSETS, outs))):
        cols = slab_columns(dx, dz)
        product = jnp.dot(s_own, n_own[:, cols], preferred_element_type=jnp.float32)
        product = product + jnp.dot(s_oth, n_oth[:, cols], preferred_element_type=jnp.float32)
        out[...] = product.astype(out.dtype)


def whole_pieces(refs):
    pieces = [ref[...] for ref in refs]
    return pieces[:3] + [jnp.concatenate(pieces[3:], axis=0)]


def forward_kernel(n_own, n_oth, *refs):
    pieces, out_ref = whole_pieces(refs[:-1]), refs[-1]
    out_ref[0] = values_of(n_own, pieces, 0)
    out_ref[1] = values_of(n_oth, pieces, 0)


def turn_kernel(index, n_own, n_oth, cot_own, cot_oth, part_ref, p0, p1, p2, p3, p4, s_own, s_oth, *outs):
    pieces = whole_pieces((p0, p1, p2, p3, p4))
    for half, (rows, cot_ref, s_ref) in enumerate(((n_own, cot_own, s_own), (n_oth, cot_oth, s_oth))):
        values = (part_ref[half] + values_of(rows, pieces, 1)) * inv_width
        gate = jax.nn.sigmoid(values)
        cot = cot_ref[0, index, :, half_columns(my_core())].astype(jnp.float32)
        s_ref[...] = (cot * (gate * (1.0 + values * (1.0 - gate)))).T.astype(jnp.bfloat16)
    gradients(n_own, n_oth, s_own[...], s_oth[...], outs, 1)


def backward_kernel(n_own, n_oth, s_own, s_oth, *outs):
    gradients(n_own, n_oth, s_own[...], s_oth[...], outs, 0)


def big_call(kernel, n_vmem, out_shape, name, flops):
    vmem = pl.BlockSpec(memory_space=pltpu.VMEM)
    return pl.pallas_call(
        kernel,
        in_specs=[vmem] * n_vmem,
        out_specs=[vmem] * len(out_shape),
        out_shape=out_shape,
        compiler_params=pltpu.CompilerParams(vmem_limit_bytes=20 * 2**20),
        cost_estimate=pl.CostEstimate(flops=flops, bytes_accessed=2**20, transcendentals=0),
        name=name,
    )


def after(value, *others):
    return lax.optimization_barrier((value, *others))[0]


def spread(piece):
    below, above = send(piece, X_UP), send(piece, X_DOWN)
    half = HALF // 2
    return piece, below, above, send(below[:half], X_UP), send(above[half:], X_DOWN)


def on_device(local_weights, outer_base, outer_momentum, batch, cotangent, step, plan):
    rows_of, width = outer_base.shape
    rate = inner_rate * inv_width
    slab, slab_bf16, slopes = f32_shape(HALF, SLAB), bf16_shape(HALF, SLAB), bf16_shape(HALF, TOK)

    half_w = f32_shape(HALF, rows_of)
    w_mine, w_sent = small_call(split_weights_kernel, 0, 1, [half_w] * 2, "split_weights")(local_weights)
    w_got = send(w_sent, C_SWAP)
    weights, own = small_call(merge_kernel, 0, 2, [slab, slab_bf16], "merge")(w_mine, w_got)
    batches = (in_hbm(batch), send(after(batch, w_got), C_SWAP))

    def sum_step(total, k):
        return total + lax.ppermute(total, "replica", REPLICA_STEPS[k])

    total = outer_in(step, plan, outer_base, local_weights, outer_momentum)
    for index in range(INNER):
        other = send(own, Z_SWAP)
        pieces = spread(own)
        other = after(other, *pieces[1:])
        if index == 0:
            other = after(other, total, batches[1])
            cots = (cotangent, send(after(cotangent, other), C_SWAP))
        pieces_other = spread(other)
        normed = [normalize(rows, index) for rows in batches]
        part = big_call(forward_kernel, 7, [f32_shape(2, TOK, HALF)], "forward", 8 * TOK * SLAB * HALF)(
            *normed, *pieces
        )[0]
        total = sum_step(after(total, other), 2 * index)
        part = after(part, total)
        s_own, s_oth, *grads_other = big_call(
            lambda *refs, index=index: turn_kernel(index, *refs),
            10,
            [slopes] * 2 + [slab] + [slab_bf16] * 3,
            "turn",
            16 * TOK * SLAB * HALF,
        )(*normed, *cots, part, *pieces_other)
        own_grad, *sent_grads = grads_other
        arrived = [send(grad, pairs) for grad, pairs in zip(sent_grads, (X_DOWN, X_UP, X_FAR))]
        sum_other = sum((piece.astype(jnp.float32) for piece in arrived), own_grad)
        grads = big_call(backward_kernel, 4, [slab] + [slab_bf16] * 3, "backward", 8 * TOK * SLAB * HALF)(
            *normed, s_own, s_oth
        )
        total = sum_step(after(total, s_own), 2 * index + 1)
        sum_other = after(sum_other, total)
        got = send(sum_other.astype(jnp.bfloat16), Z_SWAP)
        below = send(grads[1], X_DOWN)
        above = send(grads[2], X_UP)
        far = send(grads[3], X_FAR)
        mine = sum((piece.astype(jnp.float32) for piece in (below, above, far)), grads[0])
        if index == 0:
            weights = weights - rate * (mine + got.astype(jnp.float32))
            own = weights.astype(jnp.bfloat16)

    new_base, new_momentum = small_call(
        outer_out_kernel, 2, 3, [f32_shape(rows_of, width), f32_shape(*outer_momentum.shape)], "outer_out"
    )(step, plan, total, outer_base, outer_momentum)

    kept, sent = small_call(finish_kernel, 0, 3, [half_w] * 2, "finish")(weights, after(mine, new_base), got)
    new_weights = small_call(join_kernel, 2, 3, [f32_shape(1, rows_of, width)], "join")(
        step, plan, new_base, kept, send(sent, C_SWAP)
    )[0]
    return (new_weights, new_base, new_momentum)


def solution(mesh):
    placed = (
        P("replica", "fsdp", None),
        P("fsdp", None),
        P(("fsdp", "replica"), None),
        P("replica", None, "fsdp", None),
        P("replica", None, "fsdp", None),
        P(),
        P(),
    )
    return jax.shard_map(
        on_device,
        mesh=mesh,
        in_specs=placed,
        out_specs=(P("replica", "fsdp", None), P("fsdp", None), P(("fsdp", "replica"), None)),
        check_vma=False,
    )
```

```python
import jax
import jax.numpy as jnp
from jax import lax
from jax.experimental import pallas as pl
from jax.experimental.pallas import tpu as pltpu
from jax.sharding import PartitionSpec as P

D = 5120
HEAD_DIM = 128
SCHED_LEN = 8
INNER = 2
TOK = 384
HALF = 256
SLAB = 640

eps_norm = 1e-06
eps_scale = 1e-06
inner_rate = 0.5
outer_rate = 0.7
outer_decay = 0.9
mix_local = 0.5
inv_width = D ** (-0.5)


def place(x, z, c):
    return (x * 2 + z) * 2 + c


PLACES = [(x, z, c) for x in range(4) for z in range(2) for c in range(2)]
X_UP = [(place(x, z, c), place((x + 1) % 4, z, c)) for x, z, c in PLACES]
X_DOWN = [(place(x, z, c), place((x - 1) % 4, z, c)) for x, z, c in PLACES]
Z_SWAP = [(place(x, z, c), place(x, 1 - z, c)) for x, z, c in PLACES]
C_SWAP = [(place(x, z, c), place(x, z, 1 - c)) for x, z, c in PLACES]


REPLICA_STEPS = [[(r, r ^ bit) for r in range(16)] for bit in (4, 8, 1, 2)]


def send(value, pairs):
    return lax.ppermute(value, "fsdp", pairs)


def in_hbm(value):
    return pltpu.with_memory_space_constraint(value, pltpu.HBM)


def normalize_kernel(rows_ref, out_ref):
    values = rows_ref[0, 0].astype(jnp.float32)
    mean_square = jnp.mean(values * values, axis=-1, keepdims=True)
    out_ref[...] = (values * lax.rsqrt(mean_square + eps_norm)).astype(jnp.bfloat16)


def normalize(batch, index):
    block = 96
    return pl.pallas_call(
        normalize_kernel,
        grid=(TOK // block,),
        in_specs=[pl.BlockSpec((1, 1, block, D), lambda i: (0, index, i, 0))],
        out_specs=pl.BlockSpec((block, D), lambda i: (i, 0)),
        out_shape=jax.ShapeDtypeStruct((TOK, D), jnp.bfloat16),
        compiler_params=pltpu.CompilerParams(vmem_limit_bytes=16 * 2**20),
        cost_estimate=pl.CostEstimate(flops=4 * TOK * D, bytes_accessed=4 * TOK * D, transcendentals=TOK),
        name="normalize",
    )(batch)


def small_call(kernel, n_smem, n_vmem, out_shape, name):
    vmem = pl.BlockSpec(memory_space=pltpu.VMEM)
    return pl.pallas_call(
        kernel,
        in_specs=[pl.BlockSpec(memory_space=pltpu.SMEM)] * n_smem + [vmem] * n_vmem,
        out_specs=[vmem] * len(out_shape),
        out_shape=out_shape,
        compiler_params=pltpu.CompilerParams(vmem_limit_bytes=8 * 2**20),
        name=name,
    )


def f32_shape(*dims):
    return jax.ShapeDtypeStruct(dims, jnp.float32)


def bf16_shape(*dims):
    return jax.ShapeDtypeStruct(dims, jnp.bfloat16)


def my_core():
    return lax.axis_index("fsdp") % 2


def half_columns(core):
    return pl.ds(pl.multiple_of(core * HALF, HALF), HALF)


def fragment_columns(step_ref, plan_ref):
    fragment = plan_ref[lax.rem(step_ref[0], SCHED_LEN)]
    return pl.ds(pl.multiple_of(fragment * HEAD_DIM, HEAD_DIM), HEAD_DIM)


def split_weights_kernel(weights_ref, w_mine, w_sent):
    core = my_core()
    for out, half in ((w_sent, 1 - core), (w_mine, core)):
        out[...] = weights_ref[0, :, half_columns(half)].T


def merge_kernel(w_mine, w_got, whole_ref, rounded_ref):
    for core in range(2):
        low, high = (w_mine, w_got) if core == 0 else (w_got, w_mine)

        @pl.when(my_core() == core)
        def _():
            whole = jnp.concatenate([low[...], high[...]], axis=1)
            whole_ref[...] = whole
            rounded_ref[...] = whole.astype(jnp.bfloat16)


def finish_kernel(w_ref, mine_ref, got_ref, kept_ref, sent_ref):
    gradient = mine_ref[...] + got_ref[...].astype(jnp.float32)
    trained = w_ref[...] - inner_rate * inv_width * gradient
    rows = kept_ref.shape[1]
    for core in range(2):
        low, high = (kept_ref, sent_ref) if core == 0 else (sent_ref, kept_ref)

        @pl.when(my_core() == core)
        def _():
            low[...] = trained[:, :rows]
            high[...] = trained[:, rows:]


def outer_in_kernel(
    step_ref, plan_ref, base_hbm, weights_hbm, momentum_hbm, out_ref, base_ref, weights_ref, momentum_ref, sems
):
    cols = fragment_columns(step_ref, plan_ref)
    copies = [
        pltpu.make_async_copy(base_hbm.at[:, cols], base_ref, sems.at[0]),
        pltpu.make_async_copy(weights_hbm.at[0, :, cols], weights_ref, sems.at[1]),
        pltpu.make_async_copy(momentum_hbm.at[:, cols], momentum_ref, sems.at[2]),
    ]
    for copy in copies:
        copy.start()
    for copy in copies:
        copy.wait()
    replicas = lax.axis_size("replica")
    pseudo_grad = base_ref[...] - weights_ref[...]
    block_scale = (jnp.max(jnp.abs(pseudo_grad), axis=1, keepdims=True) + eps_scale).astype(jnp.bfloat16)
    block_scale = block_scale.astype(jnp.float32)
    codes = (pseudo_grad / block_scale).astype(jnp.bfloat16).astype(jnp.float32)
    products = codes * block_scale * ((1.0 + outer_decay) / replicas)
    moment = outer_decay**2 * momentum_ref[...]
    share = momentum_ref.shape[0]
    mine = lax.axis_index("replica")
    for k in range(replicas):
        rows = slice(k * share, (k + 1) * share)
        out_ref[rows] = products[rows] + jnp.where(mine == k, moment, 0.0)


def outer_in(step, plan, base, weights, momentum):
    rows, share = base.shape[0], momentum.shape[0]
    smem, hbm = pl.BlockSpec(memory_space=pltpu.SMEM), pl.BlockSpec(memory_space=pl.ANY)
    return pl.pallas_call(
        outer_in_kernel,
        in_specs=[smem] * 2 + [hbm] * 3,
        out_specs=pl.BlockSpec(memory_space=pltpu.VMEM),
        out_shape=f32_shape(rows, HEAD_DIM),
        scratch_shapes=[pltpu.VMEM((size, HEAD_DIM), jnp.float32) for size in (rows, rows, share)]
        + [pltpu.SemaphoreType.DMA((3,))],
        compiler_params=pltpu.CompilerParams(vmem_limit_bytes=8 * 2**20),
        name="outer_in",
    )(step, plan, in_hbm(base), in_hbm(weights), in_hbm(momentum))


def outer_out_kernel(step_ref, plan_ref, total_ref, base_ref, momentum_ref, new_base_ref, new_momentum_ref):
    cols = fragment_columns(step_ref, plan_ref)
    rate = outer_rate * 1024.0 / (1024.0 + jnp.full((1, HEAD_DIM), step_ref[0], jnp.int32).astype(jnp.float32))
    new_base_ref[...] = base_ref[...]
    new_base_ref[:, cols] = base_ref[:, cols] - rate * total_ref[...]
    share = momentum_ref.shape[0]
    mine = lax.axis_index("replica")
    total = jnp.zeros((share, HEAD_DIM), jnp.float32)
    for k in range(lax.axis_size("replica")):
        total = jnp.where(mine == k, total_ref[k * share : (k + 1) * share], total)
    moment = momentum_ref[:, cols]
    average = (total - outer_decay**2 * moment) * (1.0 / (1.0 + outer_decay))
    new_momentum_ref[...] = momentum_ref[...]
    new_momentum_ref[:, cols] = outer_decay * moment + average


def join_kernel(step_ref, plan_ref, base_ref, mine_ref, other_ref, out_ref):
    core = my_core()
    out_ref[0, :, half_columns(core)] = mine_ref[...].T
    out_ref[0, :, half_columns(1 - core)] = other_ref[...].T
    cols = fragment_columns(step_ref, plan_ref)
    out_ref[0, :, cols] = mix_local * out_ref[0, :, cols] + (1.0 - mix_local) * base_ref[:, cols]


OFFSETS = (0, -1, 1, 2)


def slab_columns(dx, dz):
    me = lax.axis_index("fsdp")
    slab = 2 * ((me // 4 + dx + 4) % 4) + ((me // 2) % 2 + dz) % 2
    return pl.ds(pl.multiple_of(slab * SLAB, SLAB), SLAB)


def values_of(rows, pieces, dz):
    total = jnp.zeros((TOK, HALF), jnp.float32)
    for dx, piece in zip(OFFSETS, pieces):
        total = total + lax.dot_general(
            rows[:, slab_columns(dx, dz)],
            piece,
            (((1,), (1,)), ((), ())),
            preferred_element_type=jnp.float32,
        )
    return total


def gradients(n_own, n_oth, s_own, s_oth, outs, dz):
    for dx, out in reversed(list(zip(OFFSETS, outs))):
        cols = slab_columns(dx, dz)
        product = jnp.dot(s_own, n_own[:, cols], preferred_element_type=jnp.float32)
        product = product + jnp.dot(s_oth, n_oth[:, cols], preferred_element_type=jnp.float32)
        out[...] = product.astype(out.dtype)


def whole_pieces(refs):
    pieces = [ref[...] for ref in refs]
    return pieces[:3] + [jnp.concatenate(pieces[3:], axis=0)]


def forward_kernel(n_own, n_oth, *refs):
    pieces, out_ref = whole_pieces(refs[:-1]), refs[-1]
    out_ref[0] = values_of(n_own, pieces, 0)
    out_ref[1] = values_of(n_oth, pieces, 0)


def turn_kernel(index, n_own, n_oth, cot_own, cot_oth, part_ref, p0, p1, p2, p3, p4, s_own, s_oth, *outs):
    pieces = whole_pieces((p0, p1, p2, p3, p4))
    for half, (rows, cot_ref, s_ref) in enumerate(((n_own, cot_own, s_own), (n_oth, cot_oth, s_oth))):
        values = (part_ref[half] + values_of(rows, pieces, 1)) * inv_width
        gate = jax.nn.sigmoid(values)
        cot = cot_ref[0, index, :, half_columns(my_core())].astype(jnp.float32)
        s_ref[...] = (cot * (gate * (1.0 + values * (1.0 - gate)))).T.astype(jnp.bfloat16)
    gradients(n_own, n_oth, s_own[...], s_oth[...], outs, 1)


def backward_kernel(n_own, n_oth, s_own, s_oth, *outs):
    gradients(n_own, n_oth, s_own[...], s_oth[...], outs, 0)


def big_call(kernel, n_vmem, out_shape, name, flops):
    vmem = pl.BlockSpec(memory_space=pltpu.VMEM)
    return pl.pallas_call(
        kernel,
        in_specs=[vmem] * n_vmem,
        out_specs=[vmem] * len(out_shape),
        out_shape=out_shape,
        compiler_params=pltpu.CompilerParams(vmem_limit_bytes=20 * 2**20),
        cost_estimate=pl.CostEstimate(flops=flops, bytes_accessed=2**20, transcendentals=0),
        name=name,
    )


def after(value, *others):
    return lax.optimization_barrier((value, *others))[0]


def spread(piece):
    below, above = send(piece, X_UP), send(piece, X_DOWN)
    half = HALF // 2
    return piece, below, above, send(below[:half], X_UP), send(above[half:], X_DOWN)


def collect(own, below, above, far):
    half = HALF // 2
    f32 = lambda v: v.astype(jnp.float32)
    from_below, from_above = send(far[:half], X_UP), send(far[half:], X_DOWN)
    above = jnp.concatenate([(f32(above[:half]) + f32(from_below)).astype(jnp.bfloat16), above[half:]], axis=0)
    below = jnp.concatenate([below[:half], (f32(below[half:]) + f32(from_above)).astype(jnp.bfloat16)], axis=0)
    return own + f32(send(above, X_UP)) + f32(send(below, X_DOWN))


def on_device(local_weights, outer_base, outer_momentum, batch, cotangent, step, plan):
    rows_of, width = outer_base.shape
    rate = inner_rate * inv_width
    slab, slab_bf16, slopes = f32_shape(HALF, SLAB), bf16_shape(HALF, SLAB), bf16_shape(HALF, TOK)

    half_w = f32_shape(HALF, rows_of)
    w_mine, w_sent = small_call(split_weights_kernel, 0, 1, [half_w] * 2, "split_weights")(local_weights)
    w_got = send(w_sent, C_SWAP)
    weights, own = small_call(merge_kernel, 0, 2, [slab, slab_bf16], "merge")(w_mine, w_got)
    batches = (in_hbm(batch), send(after(batch, w_got), C_SWAP))

    def sum_step(total, k):
        return total + lax.ppermute(total, "replica", REPLICA_STEPS[k])

    total = outer_in(step, plan, outer_base, local_weights, outer_momentum)
    for index in range(INNER):
        other = send(own, Z_SWAP)
        pieces = spread(own)
        other = after(other, *pieces[1:])
        if index == 0:
            other = after(other, total, batches[1])
            cots = (cotangent, send(after(cotangent, other), C_SWAP))
        pieces_other = spread(other)
        normed = [normalize(rows, index) for rows in batches]
        part = big_call(forward_kernel, 7, [f32_shape(2, TOK, HALF)], "forward", 8 * TOK * SLAB * HALF)(
            *normed, *pieces
        )[0]
        total = sum_step(after(total, other), 2 * index)
        part = after(part, total)
        s_own, s_oth, *grads_other = big_call(
            lambda *refs, index=index: turn_kernel(index, *refs),
            10,
            [slopes] * 2 + [slab] + [slab_bf16] * 3,
            "turn",
            16 * TOK * SLAB * HALF,
        )(*normed, *cots, part, *pieces_other)
        sum_other = collect(*grads_other)
        grads = big_call(backward_kernel, 4, [slab] + [slab_bf16] * 3, "backward", 8 * TOK * SLAB * HALF)(
            *normed, s_own, s_oth
        )
        total = sum_step(after(total, s_own), 2 * index + 1)
        sum_other = after(sum_other, total)
        got = send(sum_other.astype(jnp.bfloat16), Z_SWAP)
        mine = collect(*grads)
        if index == 0:
            weights = weights - rate * (mine + got.astype(jnp.float32))
            own = weights.astype(jnp.bfloat16)

    new_base, new_momentum = small_call(
        outer_out_kernel, 2, 3, [f32_shape(rows_of, width), f32_shape(*outer_momentum.shape)], "outer_out"
    )(step, plan, total, outer_base, outer_momentum)

    kept, sent = small_call(finish_kernel, 0, 3, [half_w] * 2, "finish")(weights, after(mine, new_base), got)
    new_weights = small_call(join_kernel, 2, 3, [f32_shape(1, rows_of, width)], "join")(
        step, plan, new_base, kept, send(sent, C_SWAP)
    )[0]
    return (new_weights, new_base, new_momentum)


def solution(mesh):
    placed = (
        P("replica", "fsdp", None),
        P("fsdp", None),
        P(("fsdp", "replica"), None),
        P("replica", None, "fsdp", None),
        P("replica", None, "fsdp", None),
        P(),
        P(),
    )
    return jax.shard_map(
        on_device,
        mesh=mesh,
        in_specs=placed,
        out_specs=(P("replica", "fsdp", None), P("fsdp", None), P(("fsdp", "replica"), None)),
        check_vma=False,
    )
```

```python
import jax
import jax.numpy as jnp
from jax import lax
from jax.experimental import pallas as pl
from jax.experimental.pallas import tpu as pltpu
from jax.sharding import PartitionSpec as P

D = 5120
HEAD_DIM = 128
SCHED_LEN = 8
INNER = 2
TOK = 384
HALF = 256
SLAB = 640

eps_norm = 1e-06
eps_scale = 1e-06
inner_rate = 0.5
outer_rate = 0.7
outer_decay = 0.9
mix_local = 0.5
inv_width = D ** (-0.5)


def place(x, z, c):
    return (x * 2 + z) * 2 + c


PLACES = [(x, z, c) for x in range(4) for z in range(2) for c in range(2)]
X_UP = [(place(x, z, c), place((x + 1) % 4, z, c)) for x, z, c in PLACES]
X_DOWN = [(place(x, z, c), place((x - 1) % 4, z, c)) for x, z, c in PLACES]
X_FAR = [(place(x, z, c), place((x + 2) % 4, z, c)) for x, z, c in PLACES]
Z_SWAP = [(place(x, z, c), place(x, 1 - z, c)) for x, z, c in PLACES]
C_SWAP = [(place(x, z, c), place(x, z, 1 - c)) for x, z, c in PLACES]


REPLICA_STEPS = [[(r, r ^ bit) for r in range(16)] for bit in (4, 8, 1, 2)]


def send(value, pairs):
    return lax.ppermute(value, "fsdp", pairs)


def in_hbm(value):
    return pltpu.with_memory_space_constraint(value, pltpu.HBM)


def normalize_kernel(rows_ref, out_ref):
    values = rows_ref[0, 0].astype(jnp.float32)
    mean_square = jnp.mean(values * values, axis=-1, keepdims=True)
    out_ref[...] = (values * lax.rsqrt(mean_square + eps_norm)).astype(jnp.bfloat16)


def normalize(batch, index):
    block = 96
    return pl.pallas_call(
        normalize_kernel,
        grid=(TOK // block,),
        in_specs=[pl.BlockSpec((1, 1, block, D), lambda i: (0, index, i, 0))],
        out_specs=pl.BlockSpec((block, D), lambda i: (i, 0)),
        out_shape=jax.ShapeDtypeStruct((TOK, D), jnp.bfloat16),
        compiler_params=pltpu.CompilerParams(vmem_limit_bytes=16 * 2**20),
        cost_estimate=pl.CostEstimate(flops=4 * TOK * D, bytes_accessed=4 * TOK * D, transcendentals=TOK),
        name="normalize",
    )(batch)


def small_call(kernel, n_smem, n_vmem, out_shape, name):
    vmem = pl.BlockSpec(memory_space=pltpu.VMEM)
    return pl.pallas_call(
        kernel,
        in_specs=[pl.BlockSpec(memory_space=pltpu.SMEM)] * n_smem + [vmem] * n_vmem,
        out_specs=[vmem] * len(out_shape),
        out_shape=out_shape,
        compiler_params=pltpu.CompilerParams(vmem_limit_bytes=8 * 2**20),
        name=name,
    )


def f32_shape(*dims):
    return jax.ShapeDtypeStruct(dims, jnp.float32)


def bf16_shape(*dims):
    return jax.ShapeDtypeStruct(dims, jnp.bfloat16)


def my_core():
    return lax.axis_index("fsdp") % 2


def half_columns(core):
    return pl.ds(pl.multiple_of(core * HALF, HALF), HALF)


def fragment_columns(step_ref, plan_ref):
    fragment = plan_ref[lax.rem(step_ref[0], SCHED_LEN)]
    return pl.ds(pl.multiple_of(fragment * HEAD_DIM, HEAD_DIM), HEAD_DIM)


def split_weights_kernel(weights_ref, w_mine, w_sent):
    core = my_core()
    for out, half in ((w_sent, 1 - core), (w_mine, core)):
        out[...] = weights_ref[0, :, half_columns(half)].T


def merge_kernel(w_mine, w_got, whole_ref, rounded_ref):
    for core in range(2):
        low, high = (w_mine, w_got) if core == 0 else (w_got, w_mine)

        @pl.when(my_core() == core)
        def _():
            whole = jnp.concatenate([low[...], high[...]], axis=1)
            whole_ref[...] = whole
            rounded_ref[...] = whole.astype(jnp.bfloat16)


def finish_kernel(w_ref, mine_ref, got_ref, kept_ref, sent_ref):
    gradient = mine_ref[...] + got_ref[...].astype(jnp.float32)
    trained = w_ref[...] - inner_rate * inv_width * gradient
    rows = kept_ref.shape[1]
    for core in range(2):
        low, high = (kept_ref, sent_ref) if core == 0 else (sent_ref, kept_ref)

        @pl.when(my_core() == core)
        def _():
            low[...] = trained[:, :rows]
            high[...] = trained[:, rows:]


def outer_in_kernel(
    step_ref, plan_ref, base_hbm, weights_hbm, momentum_hbm, out_ref, base_ref, weights_ref, momentum_ref, sems
):
    cols = fragment_columns(step_ref, plan_ref)
    copies = [
        pltpu.make_async_copy(base_hbm.at[:, cols], base_ref, sems.at[0]),
        pltpu.make_async_copy(weights_hbm.at[0, :, cols], weights_ref, sems.at[1]),
        pltpu.make_async_copy(momentum_hbm.at[:, cols], momentum_ref, sems.at[2]),
    ]
    for copy in copies:
        copy.start()
    for copy in copies:
        copy.wait()
    replicas = lax.axis_size("replica")
    pseudo_grad = base_ref[...] - weights_ref[...]
    block_scale = (jnp.max(jnp.abs(pseudo_grad), axis=1, keepdims=True) + eps_scale).astype(jnp.bfloat16)
    block_scale = block_scale.astype(jnp.float32)
    codes = (pseudo_grad / block_scale).astype(jnp.bfloat16).astype(jnp.float32)
    products = codes * block_scale * ((1.0 + outer_decay) / replicas)
    moment = outer_decay**2 * momentum_ref[...]
    share = momentum_ref.shape[0]
    mine = lax.axis_index("replica")
    for k in range(replicas):
        rows = slice(k * share, (k + 1) * share)
        out_ref[rows] = products[rows] + jnp.where(mine == k, moment, 0.0)


def outer_in(step, plan, base, weights, momentum):
    rows, share = base.shape[0], momentum.shape[0]
    smem, hbm = pl.BlockSpec(memory_space=pltpu.SMEM), pl.BlockSpec(memory_space=pl.ANY)
    return pl.pallas_call(
        outer_in_kernel,
        in_specs=[smem] * 2 + [hbm] * 3,
        out_specs=pl.BlockSpec(memory_space=pltpu.VMEM),
        out_shape=f32_shape(rows, HEAD_DIM),
        scratch_shapes=[pltpu.VMEM((size, HEAD_DIM), jnp.float32) for size in (rows, rows, share)]
        + [pltpu.SemaphoreType.DMA((3,))],
        compiler_params=pltpu.CompilerParams(vmem_limit_bytes=8 * 2**20),
        name="outer_in",
    )(step, plan, in_hbm(base), in_hbm(weights), in_hbm(momentum))


def outer_out_kernel(step_ref, plan_ref, total_ref, base_ref, momentum_ref, new_base_ref, new_momentum_ref):
    cols = fragment_columns(step_ref, plan_ref)
    rate = outer_rate * 1024.0 / (1024.0 + jnp.full((1, HEAD_DIM), step_ref[0], jnp.int32).astype(jnp.float32))
    new_base_ref[...] = base_ref[...]
    new_base_ref[:, cols] = base_ref[:, cols] - rate * total_ref[...]
    share = momentum_ref.shape[0]
    mine = lax.axis_index("replica")
    total = jnp.zeros((share, HEAD_DIM), jnp.float32)
    for k in range(lax.axis_size("replica")):
        total = jnp.where(mine == k, total_ref[k * share : (k + 1) * share], total)
    moment = momentum_ref[:, cols]
    average = (total - outer_decay**2 * moment) * (1.0 / (1.0 + outer_decay))
    new_momentum_ref[...] = momentum_ref[...]
    new_momentum_ref[:, cols] = outer_decay * moment + average


def join_kernel(step_ref, plan_ref, base_ref, mine_ref, other_ref, out_ref):
    core = my_core()
    out_ref[0, :, half_columns(core)] = mine_ref[...].T
    out_ref[0, :, half_columns(1 - core)] = other_ref[...].T
    cols = fragment_columns(step_ref, plan_ref)
    out_ref[0, :, cols] = mix_local * out_ref[0, :, cols] + (1.0 - mix_local) * base_ref[:, cols]


OFFSETS = (0, -1, 1, 2)


def slab_columns(dx, dz):
    me = lax.axis_index("fsdp")
    slab = 2 * ((me // 4 + dx + 4) % 4) + ((me // 2) % 2 + dz) % 2
    return pl.ds(pl.multiple_of(slab * SLAB, SLAB), SLAB)


def values_of(rows, pieces, dz):
    total = jnp.zeros((TOK, HALF), jnp.float32)
    for dx, piece in zip(OFFSETS, pieces):
        total = total + lax.dot_general(
            rows[:, slab_columns(dx, dz)],
            piece,
            (((1,), (1,)), ((), ())),
            preferred_element_type=jnp.float32,
        )
    return total


def gradients(n_own, n_oth, s_own, s_oth, outs, dz):
    for dx, out in reversed(list(zip(OFFSETS, outs))):
        cols = slab_columns(dx, dz)
        product = jnp.dot(s_own, n_own[:, cols], preferred_element_type=jnp.float32)
        product = product + jnp.dot(s_oth, n_oth[:, cols], preferred_element_type=jnp.float32)
        out[...] = product.astype(out.dtype)


def whole_pieces(refs):
    pieces = [ref[...] for ref in refs]
    return pieces[:3] + [jnp.concatenate(pieces[3:], axis=0)]


def forward_kernel(n_own, n_oth, *refs):
    pieces, out_ref = whole_pieces(refs[:-1]), refs[-1]
    out_ref[0] = values_of(n_own, pieces, 0)
    out_ref[1] = values_of(n_oth, pieces, 0)


def turn_kernel(index, n_own, n_oth, cot_own, cot_oth, part_ref, p0, p1, p2, p3, p4, s_own, s_oth, *outs):
    pieces = whole_pieces((p0, p1, p2, p3, p4))
    for half, (rows, cot_ref, s_ref) in enumerate(((n_own, cot_own, s_own), (n_oth, cot_oth, s_oth))):
        values = (part_ref[half] + values_of(rows, pieces, 1)) * inv_width
        gate = jax.nn.sigmoid(values)
        cot = cot_ref[0, index, :, half_columns(my_core())].astype(jnp.float32)
        s_ref[...] = (cot * (gate * (1.0 + values * (1.0 - gate)))).T.astype(jnp.bfloat16)
    gradients(n_own, n_oth, s_own[...], s_oth[...], outs, 1)


def backward_kernel(n_own, n_oth, s_own, s_oth, *outs):
    gradients(n_own, n_oth, s_own[...], s_oth[...], outs, 0)


def big_call(kernel, n_vmem, out_shape, name, flops):
    vmem = pl.BlockSpec(memory_space=pltpu.VMEM)
    return pl.pallas_call(
        kernel,
        in_specs=[vmem] * n_vmem,
        out_specs=[vmem] * len(out_shape),
        out_shape=out_shape,
        compiler_params=pltpu.CompilerParams(vmem_limit_bytes=20 * 2**20),
        cost_estimate=pl.CostEstimate(flops=flops, bytes_accessed=2**20, transcendentals=0),
        name=name,
    )


def after(value, *others):
    return lax.optimization_barrier((value, *others))[0]


def spread(piece):
    below, above = send(piece, X_UP), send(piece, X_DOWN)
    half = HALF // 2
    return piece, below, above, send(below[:half], X_UP), send(above[half:], X_DOWN)


def on_device(local_weights, outer_base, outer_momentum, batch, cotangent, step, plan):
    rows_of, width = outer_base.shape
    rate = inner_rate * inv_width
    slab, slab_bf16, slopes = f32_shape(HALF, SLAB), bf16_shape(HALF, SLAB), bf16_shape(HALF, TOK)

    half_w = f32_shape(HALF, rows_of)
    w_mine, w_sent = small_call(split_weights_kernel, 0, 1, [half_w] * 2, "split_weights")(local_weights)
    w_got = send(w_sent, C_SWAP)
    weights, own = small_call(merge_kernel, 0, 2, [slab, slab_bf16], "merge")(w_mine, w_got)
    batches = (in_hbm(batch), send(after(batch, w_got), C_SWAP))

    def sum_step(total, k):
        return total + lax.ppermute(total, "replica", REPLICA_STEPS[k])

    total = outer_in(step, plan, outer_base, local_weights, outer_momentum)
    for index in range(INNER):
        other = send(own, Z_SWAP)
        pieces = own, send(own, X_UP), send(own, X_DOWN), send(own, X_FAR)
        other = after(other, *pieces[1:])
        if index == 0:
            other = after(other, total, batches[1])
            cots = (cotangent, send(after(cotangent, other), C_SWAP))
        pieces_other = spread(other)
        normed = [normalize(rows, index) for rows in batches]
        part = big_call(forward_kernel, 6, [f32_shape(2, TOK, HALF)], "forward", 8 * TOK * SLAB * HALF)(
            *normed, *pieces
        )[0]
        total = sum_step(after(total, other), 2 * index)
        part = after(part, total)
        s_own, s_oth, *grads_other = big_call(
            lambda *refs, index=index: turn_kernel(index, *refs),
            10,
            [slopes] * 2 + [slab] + [slab_bf16] * 3,
            "turn",
            16 * TOK * SLAB * HALF,
        )(*normed, *cots, part, *pieces_other)
        own_grad, *sent_grads = grads_other
        arrived = [send(grad, pairs) for grad, pairs in zip(sent_grads, (X_DOWN, X_UP, X_FAR))]
        sum_other = sum((piece.astype(jnp.float32) for piece in arrived), own_grad)
        grads = big_call(backward_kernel, 4, [slab] + [slab_bf16] * 3, "backward", 8 * TOK * SLAB * HALF)(
            *normed, s_own, s_oth
        )
        total = sum_step(after(total, s_own), 2 * index + 1)
        sum_other = after(sum_other, total)
        got = send(sum_other.astype(jnp.bfloat16), Z_SWAP)
        below = send(grads[1], X_DOWN)
        above = send(grads[2], X_UP)
        far = send(grads[3], X_FAR)
        mine = sum((piece.astype(jnp.float32) for piece in (below, above, far)), grads[0])
        if index == 0:
            weights = weights - rate * (mine + got.astype(jnp.float32))
            own = weights.astype(jnp.bfloat16)

    new_base, new_momentum = small_call(
        outer_out_kernel, 2, 3, [f32_shape(rows_of, width), f32_shape(*outer_momentum.shape)], "outer_out"
    )(step, plan, total, outer_base, outer_momentum)

    kept, sent = small_call(finish_kernel, 0, 3, [half_w] * 2, "finish")(weights, after(mine, new_base), got)
    new_weights = small_call(join_kernel, 2, 3, [f32_shape(1, rows_of, width)], "join")(
        step, plan, new_base, kept, send(sent, C_SWAP)
    )[0]
    return (new_weights, new_base, new_momentum)


def solution(mesh):
    placed = (
        P("replica", "fsdp", None),
        P("fsdp", None),
        P(("fsdp", "replica"), None),
        P("replica", None, "fsdp", None),
        P("replica", None, "fsdp", None),
        P(),
        P(),
    )
    return jax.shard_map(
        on_device,
        mesh=mesh,
        in_specs=placed,
        out_specs=(P("replica", "fsdp", None), P("fsdp", None), P(("fsdp", "replica"), None)),
        check_vma=False,
    )
```
